32 devices in a mesh: row: 8 (over z, x), col: 4 (over y, core).
Axes of the slice: x: 2, y: 2, z: 4, core: 2. Of those that a mesh axis runs over, the one named last changes fastest.
Arguments:
- hamiltonian: float32 [16384, 16384], P('row', 'col'), may hold values from -64 to 64, as said below
Outputs:
- updated: float32 [16384, 16384], P('row', 'col')
The draws below stay inside these ranges and needn't reach their ends.
Inputs may be any that keep to these rules, and one draw needn't show every extreme that they name: hamiltonian is symmetric as a matrix in natural order.
All inputs are finite; a program needn't handle non-finite values.
Results may differ from the reference program's by a relative error of at most 0.0001.
Values sent between devices are 32-bit elements; how exact they have to be, the bound alone decides.
No kernel may reach another device: no remote copies, remote signals or barrier semaphores. Data moves between devices by JAX's collectives and lax.ppermute only.
A program may use at most 192 MiB of HBM per device.

```python
import jax
import jax.numpy as jnp
from jax import lax

N = 16384
NB = 128
PANELS = 2
GRID_ROWS = 8
GRID_COLS = 4


def draw_hamiltonian(key, part):
    first = jax.random.fold_in(jax.random.fold_in(key, 11), 0)
    raw = jnp.clip(jax.random.normal(first, (N, N), jnp.float32), -5.0, 5.0)
    blocks = jnp.arange(N) // NB
    scale = 0.5 + (blocks % GRID_ROWS).astype(jnp.float32) / max(GRID_ROWS - 1, 1)
    symmetric = (raw + raw.T) * 0.7071 * scale[:, None] * scale[None, :]
    shaped = symmetric.reshape(N // (GRID_ROWS * NB), GRID_ROWS, NB, N // (GRID_COLS * NB), GRID_COLS, NB)
    return shaped.transpose(1, 0, 2, 4, 3, 5).reshape(N, N)


def setup_inputs(seed: int = 0) -> dict:
    seeds = jax.random.split(jax.random.key(seed), 2)
    return {
        "hamiltonian": draw_hamiltonian(jax.random.fold_in(seeds[1], 71), 0),
    }


HIGH = lax.Precision.HIGHEST

def to_natural(matrix):
    shaped = matrix.reshape(GRID_ROWS, N // (GRID_ROWS * NB), NB, GRID_COLS, N // (GRID_COLS * NB), NB)
    return shaped.transpose(1, 0, 2, 4, 3, 5).reshape(N, N)

def to_stored(matrix):
    shaped = matrix.reshape(N // (GRID_ROWS * NB), GRID_ROWS, NB, N // (GRID_COLS * NB), GRID_COLS, NB)
    return shaped.transpose(1, 0, 2, 4, 3, 5).reshape(N, N)

def panel_step(matrix, panel):
    start = panel * NB
    position = jnp.arange(N)
    columns = matrix[:, start:start + NB]
    columns = jnp.where((position >= start + NB)[:, None], columns, jnp.float32(0.0))
    gram = jnp.dot(columns.T, columns, precision=HIGH)
    factor = jnp.linalg.cholesky(gram)
    reflect = lax.linalg.triangular_solve(factor, columns, left_side=False, lower=True, transpose_a=True)
    product = jnp.dot(matrix, reflect, precision=HIGH)
    coupling = jnp.dot(reflect.T, product, precision=HIGH)
    update = 2.0 * product - 2.0 * jnp.dot(reflect, coupling, precision=HIGH)
    return matrix - jnp.dot(reflect, update.T, precision=HIGH) - jnp.dot(update, reflect.T, precision=HIGH)

def reference(hamiltonian):
    matrix = to_natural(hamiltonian)
    for panel in range(PANELS):
        matrix = panel_step(matrix, panel)
    return to_stored(matrix)
```

```python
import functools

import jax
import jax.numpy as jnp
from jax import lax
from jax.experimental import pallas as pl
from jax.experimental.pallas import tpu as pltpu
from jax.sharding import PartitionSpec as P

NB = 128
PANELS = 2
CORES = 2
HIGH = lax.Precision.HIGHEST
BF16 = jnp.bfloat16
F32 = jnp.float32
AXES = ("row", "col")


def contract(left, right, left_dim, right_dim):
    return lax.dot_general(left, right, (((left_dim,), (right_dim,)), ((), ())), precision=HIGH)


def split(x):
    high = lax.reduce_precision(x, exponent_bits=8, mantissa_bits=7)
    return high.astype(BF16), (x - high).astype(BF16)


def tile_rows(rows):
    return 256 if rows % 256 == 0 else rows


def product_kernel(a_ref, p_ref, out_ref):
    a = a_ref[...]
    high = a.astype(BF16)
    low = (a - high.astype(F32)).astype(BF16)
    p = p_ref[...]
    both = jnp.dot(high, p, preferred_element_type=F32) + jnp.dot(low, p, preferred_element_type=F32)
    out_ref[...] = both[:, :NB] + both[:, NB:]


def product(matrix, panel):
    rows, cols = matrix.shape
    tile = tile_rows(rows)
    return pl.pallas_call(
        product_kernel,
        grid=(rows // tile,),
        in_specs=[
            pl.BlockSpec((tile, cols), lambda i: (i, 0)),
            pl.BlockSpec((cols, 2 * NB), lambda i: (0, 0)),
        ],
        out_specs=pl.BlockSpec((tile, NB), lambda i: (i, 0)),
        out_shape=jax.ShapeDtypeStruct((rows, NB), F32),
        compiler_params=pltpu.CompilerParams(vmem_limit_bytes=40 * 1024 * 1024),
        cost_estimate=pl.CostEstimate(
            flops=8 * rows * cols * NB, bytes_accessed=4 * rows * cols, transcendentals=0
        ),
        name="product",
    )(matrix, jnp.concatenate(split(panel), axis=1))


def update_kernel(a_ref, u_ref, v_ref, out_ref):
    cols = a_ref.shape[1]
    step = 512 if cols % 512 == 0 else cols
    u = u_ref[...]
    for first in range(0, cols, step):
        part = lax.dot_general(
            u, v_ref[first : first + step, :], (((1,), (1,)), ((), ())), preferred_element_type=F32
        )
        out_ref[:, first : first + step] = a_ref[:, first : first + step] - part


def subtract(matrix, left, right):
    rows, cols = matrix.shape
    tile = tile_rows(rows)
    left_high, left_low = split(left)
    right_high, right_low = split(right)
    u = jnp.concatenate([left_high, left_high, left_low], axis=1)
    v = jnp.concatenate([right_high, right_low, right_high], axis=1)
    depth = u.shape[1]
    return pl.pallas_call(
        update_kernel,
        grid=(rows // tile,),
        in_specs=[
            pl.BlockSpec((tile, cols), lambda i: (i, 0)),
            pl.BlockSpec((tile, depth), lambda i: (i, 0)),
            pl.BlockSpec((cols, depth), lambda i: (0, 0)),
        ],
        out_specs=pl.BlockSpec((tile, cols), lambda i: (i, 0)),
        out_shape=jax.ShapeDtypeStruct((rows, cols), F32),
        compiler_params=pltpu.CompilerParams(vmem_limit_bytes=48 * 1024 * 1024),
        cost_estimate=pl.CostEstimate(
            flops=2 * rows * cols * depth, bytes_accessed=8 * rows * cols, transcendentals=0
        ),
        name="subtract",
    )(matrix, u, v)


class Grid:
    def __init__(self):
        self.rows = lax.axis_size("row")
        self.cols = lax.axis_size("col")
        self.row = lax.axis_index("row")
        self.col = lax.axis_index("col")
        self.width = self.cols // CORES
        self.depth = self.rows // self.width
        self.sources = self.rows // self.cols
        self.z = self.row // self.width
        self.x = self.row % self.width

    def device(self, z, x, col):
        return (z * self.width + x) * self.cols + col

    def send(self, value, pairs):
        return lax.ppermute(value, AXES, pairs)

    def swap(self, value, axis, bit):
        size = lax.axis_size(axis)
        return lax.ppermute(value, axis, [(i, i ^ bit) for i in range(size)])

    def add_over(self, value, axis, bit):
        while bit < lax.axis_size(axis):
            value = value + self.swap(value, axis, bit)
            bit *= 2
        return value

    def join_cores(self, half):
        other = self.swap(half, "col", 1)
        first = self.col % CORES == 0
        return jnp.concatenate([jnp.where(first, half, other), jnp.where(first, other, half)], axis=0)

    def own_half(self, value):
        half = value.shape[0] // CORES
        return lax.dynamic_slice_in_dim(value, self.col % CORES * half, half, axis=0)

    def other_half(self, value):
        half = value.shape[0] // CORES
        return lax.dynamic_slice_in_dim(value, (1 - self.col % CORES) * half, half, axis=0)

    def sum_half(self, value):
        mine = self.own_half(value) + self.swap(self.other_half(value), "col", 1)
        return self.add_over(mine, "col", CORES)

    def from_chip_zero(self, value):
        half = self.own_half(value)
        total = jnp.where(self.col < CORES, half, jnp.zeros_like(half))
        for y in range(1, self.cols // CORES):
            pairs = [
                (r * self.cols + core, r * self.cols + y * CORES + core)
                for r in range(self.rows)
                for core in range(CORES)
            ]
            total = total + self.send(half, pairs)
        return self.join_cores(total)

    def to_columns(self, item, chunks):
        rows = item.shape[0]
        size = rows // chunks
        parts = [self.gather(item[i * size : (i + 1) * size]) for i in range(chunks)]
        return jnp.concatenate(parts, axis=0)

    def gather(self, item):
        wide, deep, cols, count = self.width, self.depth, self.cols, self.sources

        def pairs(moves):
            found = []
            for col in range(cols):
                mirror = col // wide == 1
                for m, n in moves:
                    z, to = (deep - 1 - m, deep - 1 - n) if mirror else (m, n)
                    found.append((self.device(z, col % wide, col), self.device(to, col % wide, col)))
            return found

        mirror = self.col // wide == 1
        place = jnp.where(mirror, deep - 1 - self.z, self.z)
        home = self.x == self.col % wide
        even = range(0, deep, 2)
        near = self.send(item, pairs([(e, e + 1) for e in even]))
        far = {
            t: self.send(item, pairs([(e, (e + 2 * t) % deep) for e in even])) for t in range(1, count)
        }
        down = {}
        for d in range(count - 1):
            value = item if d == 0 else far[count - d]
            down[d] = self.send(value, pairs([(e, e - 1) for e in even if e >= 2 and e + 2 * d < deep]))
        up = {t: self.send(far[t], pairs([(e, e + 1) for e in even if e >= 2 * t])) for t in far}
        relative = [jnp.where(place % 2 == 0, item, near)]
        for t in range(1, count):
            relative.append(far[t] + up[t] + down[count - 1 - t])
        whole = []
        for value in relative:
            crossed = jnp.zeros_like(value)
            for d in range(1, wide):
                moves = [
                    (self.device(z, col % wide, col), self.device(z, (col + d) % wide, col))
                    for z in range(deep)
                    for col in range(cols)
                ]
                crossed = crossed + self.send(value, moves)
            whole.append(jnp.where(home, value, crossed))
        own = self.z // 2
        slots = []
        for j in range(count):
            t = jnp.where(mirror, j - own, own - j) % count
            slots.append(lax.select_n(t, *whole) if count > 2 else jnp.where(t == 0, whole[0], whole[1]))
        shaped = [s.reshape(-1, 1, NB, s.shape[1]) for s in slots]
        return jnp.concatenate(shaped, axis=1).reshape(-1, item.shape[1])


def inverse_factor(gram):
    factor = jnp.linalg.cholesky(gram)
    eye = jnp.eye(NB, dtype=F32)
    return lax.linalg.triangular_solve(factor, eye, left_side=True, lower=True).T


def body(matrix):
    grid = Grid()
    local_rows, local_cols = matrix.shape
    row_slot = jnp.arange(local_rows, dtype=jnp.int32)
    col_slot = jnp.arange(local_cols, dtype=jnp.int32)
    natural_rows = ((row_slot // NB * grid.rows + grid.row) * NB + row_slot % NB)[:, None]
    natural_cols = ((col_slot // NB * grid.cols + grid.col) * NB + col_slot % NB)[:, None]
    zero = jnp.float32(0.0)

    def below(value, natural, panel):
        return jnp.where(natural >= (panel + 1) * NB, value, zero)

    def block_one(value):
        return jnp.where(grid.row == 1, value[:NB], zero)

    mine = matrix[:, :NB]
    other = grid.swap(mine, "col", 1)
    first = grid.col % CORES == 0
    p0 = grid.from_chip_zero(jnp.where(first, mine, other))
    p0 = below(p0, natural_rows, 0)
    p0c = grid.to_columns(p0, 2)
    small = grid.add_over(jnp.concatenate([contract(p0, p0, 0, 0), block_one(p0)], axis=0), "row", 1)
    t0 = inverse_factor(small[:NB])
    p0_one = small[NB:]

    later = zero * p0c[0, 0]
    b1 = grid.from_chip_zero(jnp.where(first, other, mine) + later)
    b1c = grid.to_columns(b1, 2)

    half = grid.sum_half(product(matrix, p0c))
    x0 = grid.join_cores(contract(half, t0, 1, 0))
    x0c = grid.to_columns(x0, 2)
    w0 = contract(p0, t0, 1, 0)
    w0c = contract(p0c, t0, 1, 0)
    small = grid.add_over(jnp.concatenate([contract(w0, x0, 0, 0), block_one(x0)], axis=0), "row", 1)
    m0, x0_one = small[:NB], small[NB:]
    w0_one = contract(p0_one, t0, 1, 0)
    both0 = jnp.concatenate([w0, x0], axis=1)
    both0c = jnp.concatenate([w0c, x0c], axis=1)

    to_w = 2.0 * x0_one.T - 4.0 * contract(m0, w0_one, 1, 1)
    coefficient = jnp.concatenate([to_w, 2.0 * w0_one.T], axis=0)
    p1 = below(b1 - contract(both0, coefficient, 1, 0), natural_rows, 1)
    p1c = below(b1c - contract(both0c, coefficient, 1, 0), natural_cols, 1)
    small = grid.add_over(contract(jnp.concatenate([both0, p1], axis=1), p1, 0, 0), "row", 1)
    w_p, x_p, gram = small[:NB], small[NB : 2 * NB], small[2 * NB :]
    t1 = inverse_factor(gram)
    correction = jnp.concatenate([2.0 * x_p - 4.0 * contract(m0, w_p, 1, 0), 2.0 * w_p], axis=0)
    half = grid.sum_half(product(matrix, p1c))
    half = half - contract(grid.own_half(both0), correction, 1, 0)
    x1 = grid.join_cores(contract(half, t1, 1, 0))
    x1c = grid.to_columns(x1, 2)
    w1 = contract(p1, t1, 1, 0)
    w1c = contract(p1c, t1, 1, 0)
    m1 = grid.add_over(contract(w1, x1, 0, 0), "row", 1)

    left0 = jnp.concatenate([2.0 * x0 - 4.0 * contract(w0, m0, 1, 0), 2.0 * w0], axis=1)
    middle = subtract(matrix, left0, both0c)
    left1 = jnp.concatenate([2.0 * x1 - 4.0 * contract(w1, m1, 1, 0), 2.0 * w1], axis=1)
    return subtract(middle, left1, jnp.concatenate([w1c, x1c], axis=1))


def solution(mesh):
    placed = (P("row", "col"),)
    return jax.shard_map(
        body, mesh=mesh, in_specs=placed, out_specs=P("row", "col"), check_vma=False
    )
```

```python
import jax
import jax.numpy as jnp
from jax import lax
from jax.experimental import pallas as pl
from jax.experimental.pallas import tpu as pltpu
from jax.sharding import PartitionSpec as P

NB = 128
PANELS = 2
CORES = 2
GROUP = 8
HIGH = lax.Precision.HIGHEST
BF16 = jnp.bfloat16
F32 = jnp.float32
AXES = ("row", "col")


def contract(left, right, left_dim, right_dim):
    return lax.dot_general(left, right, (((left_dim,), (right_dim,)), ((), ())), precision=HIGH)


def tile_rows(rows):
    return 512 if rows % 512 == 0 else rows


def halves(value):
    high = value.astype(BF16)
    return high, (value - high.astype(F32)).astype(BF16)


def product_kernel(a_ref, p_ref, *refs):
    out_ref, both = refs[-2:]

    @pl.when(pl.program_id(0) == 0)
    def _():
        high, low = halves(p_ref[...])
        both[:, :NB] = high
        both[:, NB:] = low

    high, low = halves(a_ref[...])
    p = both[...]
    total = jnp.dot(high, p, preferred_element_type=F32) + jnp.dot(low, p, preferred_element_type=F32)
    total = total[:, :NB] + total[:, NB:]
    out_ref[...] = total if len(refs) == 2 else refs[0][...] + total


def product(matrix, panel, index, before=()):
    rows = matrix.shape[0]
    cols = panel.shape[0]
    tile = tile_rows(rows)
    piece = pl.BlockSpec((tile, NB), lambda i: (i, 0))
    return pl.pallas_call(
        product_kernel,
        grid=(rows // tile,),
        in_specs=[
            pl.BlockSpec((tile, cols), lambda i: (i, index)),
            pl.BlockSpec((cols, NB), lambda i: (0, 0)),
            *[piece for _ in before],
        ],
        out_specs=piece,
        out_shape=jax.ShapeDtypeStruct((rows, NB), F32),
        scratch_shapes=[pltpu.VMEM((cols, 2 * NB), BF16)],
        compiler_params=pltpu.CompilerParams(vmem_limit_bytes=40 * 1024 * 1024),
        cost_estimate=pl.CostEstimate(
            flops=8 * rows * cols * NB, bytes_accessed=4 * rows * cols, transcendentals=0
        ),
        name="product",
    )(matrix, panel, *before)


def subtract_kernel(a_ref, left_w, left_y, right_w, right_y, *refs):
    out_ref, right = refs[-2:]

    @pl.when(pl.program_id(0) == 0)
    def _():
        for place, ref in ((0, right_w), (3, right_y)):
            high, low = halves(ref[...])
            right[:, place * NB : (place + 1) * NB] = high
            right[:, (place + 1) * NB : (place + 2) * NB] = low
            right[:, (place + 2) * NB : (place + 3) * NB] = high

    parts = []
    for ref in (left_w, left_y):
        high, low = halves(ref[...])
        parts += [high, high, low]
    left = jnp.concatenate(parts, axis=1)
    cols = a_ref.shape[1]
    step = 512 if cols % 512 == 0 else cols
    for first in range(0, cols, step):
        part = lax.dot_general(
            left, right[first : first + step, :], (((1,), (1,)), ((), ())), preferred_element_type=F32
        )
        out_ref[:, first : first + step] = a_ref[:, first : first + step] - part


def subtract(matrix, index, left, right, out_cols, out_index, into=()):
    rows = matrix.shape[0]
    cols = right[0].shape[0]
    tile = tile_rows(rows)
    return pl.pallas_call(
        subtract_kernel,
        grid=(rows // tile,),
        in_specs=[
            pl.BlockSpec((tile, cols), lambda i: (i, index)),
            *[pl.BlockSpec((tile, NB), lambda i: (i, 0))] * 2,
            *[pl.BlockSpec((cols, NB), lambda i: (0, 0))] * 2,
            *[pl.BlockSpec(memory_space=pl.ANY) for _ in into],
        ],
        out_specs=pl.BlockSpec((tile, cols), lambda i: (i, out_index)),
        out_shape=jax.ShapeDtypeStruct((rows, out_cols), F32),
        scratch_shapes=[pltpu.VMEM((cols, 6 * NB), BF16)],
        input_output_aliases={5: 0} if into else {},
        compiler_params=pltpu.CompilerParams(vmem_limit_bytes=48 * 1024 * 1024),
        cost_estimate=pl.CostEstimate(
            flops=12 * rows * cols * NB, bytes_accessed=8 * rows * cols, transcendentals=0
        ),
        name="subtract",
    )(matrix, *left, *right, *into)


def factor_kernel(gram_ref, out_ref, rest, side):
    rest[...] = gram_ref[...]
    down = lax.broadcasted_iota(jnp.int32, (NB, NB), 0)
    side[...] = jnp.where(down == lax.broadcasted_iota(jnp.int32, (NB, NB), 1), 1.0, 0.0)
    for first in range(0, NB, GROUP):
        end = first + GROUP
        rows = [rest[i : i + 1, :] for i in range(first, end)]
        sides = [side[i : i + 1, :] for i in range(first, end)]
        corner = {
            (i, j): jnp.broadcast_to(rows[i][:, first + j : first + j + 1], (1, NB))
            for i in range(GROUP)
            for j in range(i + 1)
        }
        for j in range(GROUP):
            pivot = corner[j, j]
            scale = lax.rsqrt(pivot)
            scale = scale * (1.5 - 0.5 * pivot * scale * scale)
            rows[j] = rows[j] * scale
            sides[j] = sides[j] * scale
            low = {i: corner[i, j] * scale for i in range(j + 1, GROUP)}
            for i in range(j + 1, GROUP):
                rows[i] = rows[i] - low[i] * rows[j]
                sides[i] = sides[i] - low[i] * sides[j]
                for k in range(j + 1, i + 1):
                    corner[i, k] = corner[i, k] - low[i] * low[k]
        upper = jnp.concatenate(rows, axis=0)
        inverse = jnp.concatenate(sides, axis=0)
        side[first:end, :] = inverse
        if end < NB:
            taken = contract(upper, jnp.concatenate([upper, inverse], axis=1), 0, 0)
            rest[end:, :] = rest[end:, :] - taken[end:, :NB]
            side[end:, :] = side[end:, :] - taken[end:, NB:]
    out_ref[...] = side[...].T


def inverse_factor(gram):
    return pl.pallas_call(
        factor_kernel,
        out_shape=jax.ShapeDtypeStruct((NB, NB), F32),
        scratch_shapes=[pltpu.VMEM((NB, NB), F32)] * 2,
        compiler_params=pltpu.CompilerParams(vmem_limit_bytes=16 * 1024 * 1024),
        cost_estimate=pl.CostEstimate(flops=4 * NB**3, bytes_accessed=8 * NB * NB, transcendentals=NB),
        name="factor",
    )(gram)


def after(value, *others):
    return value + jnp.float32(0.0) * sum(other[0, 0] for other in others)


class Grid:
    def __init__(self):
        self.rows = lax.axis_size("row")
        self.cols = lax.axis_size("col")
        self.row = lax.axis_index("row")
        self.col = lax.axis_index("col")
        self.width = self.cols // CORES
        self.depth = self.rows // self.width
        self.sources = self.rows // self.cols
        self.z = self.row // self.width
        self.x = self.row % self.width

    def device(self, z, x, col):
        return (z * self.width + x) * self.cols + col

    def send(self, value, pairs):
        return lax.ppermute(value, AXES, pairs)

    def swap(self, value, axis, bit):
        size = lax.axis_size(axis)
        return lax.ppermute(value, axis, [(i, i ^ bit) for i in range(size)])

    def add_over(self, value, axis, bit):
        while bit < lax.axis_size(axis):
            value = value + self.swap(value, axis, bit)
            bit *= 2
        return value

    def join_cores(self, half):
        other = self.swap(half, "col", 1)
        first = self.col % CORES == 0
        return jnp.concatenate([jnp.where(first, half, other), jnp.where(first, other, half)], axis=0)

    def own_half(self, value):
        half = value.shape[0] // CORES
        return lax.dynamic_slice_in_dim(value, self.col % CORES * half, half, axis=0)

    def other_half(self, value):
        half = value.shape[0] // CORES
        return lax.dynamic_slice_in_dim(value, (1 - self.col % CORES) * half, half, axis=0)

    def sum_half(self, value):
        mine = self.own_half(value) + self.swap(self.other_half(value), "col", 1)
        return self.add_over(mine, "col", CORES)

    def from_chip_zero(self, value):
        half = self.own_half(value)
        total = jnp.where(self.col < CORES, half, jnp.zeros_like(half))
        for y in range(1, self.cols // CORES):
            pairs = [
                (r * self.cols + core, r * self.cols + y * CORES + core)
                for r in range(self.rows)
                for core in range(CORES)
            ]
            total = total + self.send(half, pairs)
        return self.join_cores(total)

    def to_columns(self, item, chunks):
        size = item.shape[0] // chunks
        return zip(*[self.gather(item[i * size : (i + 1) * size]) for i in range(chunks)])

    def gather(self, item):
        wide, deep, cols, count = self.width, self.depth, self.cols, self.sources

        def pairs(moves):
            found = []
            for col in range(cols):
                mirror = col // wide == 1
                for m, n in moves:
                    z, to = (deep - 1 - m, deep - 1 - n) if mirror else (m, n)
                    found.append((self.device(z, col % wide, col), self.device(to, col % wide, col)))
            return found

        mirror = self.col // wide == 1
        place = jnp.where(mirror, deep - 1 - self.z, self.z)
        home = self.x == self.col % wide
        even = range(0, deep, 2)
        near = self.send(item, pairs([(e, e + 1) for e in even]))
        far = {
            t: self.send(item, pairs([(e, (e + 2 * t) % deep) for e in even])) for t in range(1, count)
        }
        down = {}
        for d in range(count - 1):
            value = item if d == 0 else far[count - d]
            down[d] = self.send(value, pairs([(e, e - 1) for e in even if e >= 2 and e + 2 * d < deep]))
        up = {t: self.send(far[t], pairs([(e, e + 1) for e in even if e >= 2 * t])) for t in far}
        relative = [jnp.where(place % 2 == 0, item, near)]
        for t in range(1, count):
            relative.append(far[t] + up[t] + down[count - 1 - t])
        whole = []
        for value in relative:
            crossed = jnp.zeros_like(value)
            for d in range(1, wide):
                moves = [
                    (self.device(z, col % wide, col), self.device(z, (col + d) % wide, col))
                    for z in range(deep)
                    for col in range(cols)
                ]
                crossed = crossed + self.send(value, moves)
            whole.append(jnp.where(home, value, crossed))
        own = self.z // 2
        slots = []
        for j in range(count):
            t = jnp.where(mirror, j - own, own - j) % count
            slots.append(lax.select_n(t, *whole) if count > 2 else jnp.where(t == 0, whole[0], whole[1]))
        shaped = [s.reshape(-1, 1, NB, s.shape[1]) for s in slots]
        return jnp.concatenate(shaped, axis=1).reshape(-1, item.shape[1]), near, relative[1]


def body(matrix):
    grid = Grid()
    local_rows, local_cols = matrix.shape
    chunks = 2
    width = local_cols // chunks
    row_slot = jnp.arange(local_rows, dtype=jnp.int32)
    col_slot = jnp.arange(local_cols, dtype=jnp.int32)
    natural_rows = ((row_slot // NB * grid.rows + grid.row) * NB + row_slot % NB)[:, None]
    natural_cols = ((col_slot // NB * grid.cols + grid.col) * NB + col_slot % NB)[:, None]
    zero = jnp.float32(0.0)

    def below(value, natural, panel):
        return jnp.where(natural >= (panel + 1) * NB, value, zero)

    def block_one(value):
        return jnp.where(grid.row == 1, value[:NB], zero)

    mine = matrix[:, :NB]
    other = grid.swap(mine, "col", 1)
    first = grid.col % CORES == 0
    p0 = below(grid.from_chip_zero(jnp.where(first, mine, other)), natural_rows, 0)
    p0c, early, late = grid.to_columns(p0, chunks)

    b1 = grid.from_chip_zero(after(jnp.where(first, other, mine), early[0]))
    (b1c,), _, b1_late = grid.to_columns(after(b1, late[-1]), 1)

    y0 = ()
    for i in range(chunks):
        y0 = (product(matrix, p0c[i], i, y0),)
        if i == 0:
            small = jnp.concatenate([contract(p0, p0, 0, 0), block_one(p0)], axis=0)
            small = grid.add_over(after(small, y0[0]), "row", 1)
    half = grid.sum_half(y0[0])
    y0 = grid.join_cores(after(half, b1_late[0]))
    y0c, early, late = grid.to_columns(y0, chunks)
    t0 = inverse_factor(small[:NB])
    p0_one = small[NB:]
    w0 = contract(p0, t0, 1, 0)
    w0c = [contract(part, t0, 1, 0) for part in p0c]
    w0_one = contract(p0_one, t0, 1, 0)
    small = grid.add_over(jnp.concatenate([contract(w0, y0, 0, 0), block_one(y0)], axis=0), "row", 1)
    m0, y0_one = contract(small[:NB], t0, 1, 0), small[NB:]

    def coupled(m, t, w, y):
        return 2.0 * contract(t, y, 0, 0) - 4.0 * contract(m, w, 1, 0), 2.0 * contract(t, w, 1, 0)

    def lefts(m, t, w, y):
        return 2.0 * contract(y, t, 1, 0) - 4.0 * contract(w, m, 1, 0), 2.0 * contract(w, t, 1, 1)

    for_w, for_y = coupled(m0, t0, w0_one.T, y0_one.T)
    p1 = below(b1 - contract(w0, for_w, 1, 0) - contract(y0, for_y, 1, 0), natural_rows, 1)
    p1c = []
    y1 = ()
    for i in range(chunks):
        here = slice(i * width, (i + 1) * width)
        part = b1c[here] - contract(w0c[i], for_w, 1, 0) - contract(y0c[i], for_y, 1, 0)
        p1c.append(below(part, natural_cols[here], 1))
        y1 = (product(matrix, p1c[i], i, y1),)
        if i == 0:
            small = jnp.concatenate([contract(side, p1, 0, 0) for side in (w0, y0, p1)], axis=0)
            small = grid.add_over(after(small, p1c[0]), "row", 1)
    t1 = inverse_factor(after(small[2 * NB :], y1[0]))
    for_w, for_y = coupled(m0, t0, small[:NB], small[NB : 2 * NB])
    half = grid.sum_half(y1[0])
    half = half - contract(grid.own_half(w0), for_w, 1, 0) - contract(grid.own_half(y0), for_y, 1, 0)
    y1 = grid.join_cores(half)
    y1c, early, late = grid.to_columns(y1, chunks)
    w1 = contract(p1, t1, 1, 0)
    w1c = [contract(part, t1, 1, 0) for part in p1c]
    m1 = contract(grid.add_over(contract(w1, y1, 0, 0), "row", 1), t1, 1, 0)

    left = lefts(m0, t0, w0, y0)
    middle = []
    for i in range(chunks):
        held = (after(left[0], (early + late)[i]), left[1])
        middle.append(subtract(matrix, i, held, (w0c[i], y0c[i]), width, 0))
    left = lefts(m1, t1, w1, y1)
    updated = ()
    for i in range(chunks):
        updated = (subtract(middle[i], 0, left, (w1c[i], y1c[i]), local_cols, i, updated),)
    return updated[0]


def solution(mesh):
    placed = (P("row", "col"),)
    return jax.shard_map(
        body, mesh=mesh, in_specs=placed, out_specs=P("row", "col"), check_vma=False
    )
```

```python
import functools

import jax
import jax.numpy as jnp
from jax import lax
from jax.experimental import pallas as pl
from jax.experimental.pallas import tpu as pltpu
from jax.sharding import PartitionSpec as P

NB = 128
PANELS = 2
CORES = 2
GROUP = 8
SCALE = 2.0**60
HIGH = lax.Precision.HIGHEST
BF16 = jnp.bfloat16
F32 = jnp.float32
AXES = ("row", "col")


def contract(left, right, left_dim, right_dim):
    return lax.dot_general(left, right, (((left_dim,), (right_dim,)), ((), ())), precision=HIGH)


def tile_rows(rows, most):
    return most if rows % most == 0 else rows


def halves(value):
    high = value.astype(BF16)
    return high, (value - high.astype(F32)).astype(BF16)


def set_panel(ref, both):
    high, low = halves(ref[...])
    both[:, :NB] = high
    both[:, NB:] = low


def set_right(refs, right):
    for place, ref in enumerate(refs):
        high, low = halves(ref[...])
        first = 3 * place * NB
        right[:, first : first + NB] = high
        right[:, first + NB : first + 2 * NB] = low
        right[:, first + 2 * NB : first + 3 * NB] = high


def left_parts(refs):
    parts = []
    for ref in refs:
        high, low = halves(ref[...])
        parts += [high, high, low]
    return jnp.concatenate(parts, axis=1)


def less(a_ref, left, right, first, step):
    part = lax.dot_general(
        left, right[first : first + step, :], (((1,), (1,)), ((), ())), preferred_element_type=F32
    )
    return a_ref[:, first : first + step] - part


def times(a, p):
    high, low = halves(a)
    total = jnp.dot(high, p, preferred_element_type=F32) + jnp.dot(low, p, preferred_element_type=F32)
    return total[:, :NB] + total[:, NB:]


def column_step(cols):
    return 512 if cols % 512 == 0 else cols


def product_kernel(count, a_ref, p_ref, *refs):
    out_ref, both = refs[-2:]

    @pl.when(pl.program_id(0) == 0)
    def _():
        set_panel(p_ref, both)

    total = times(a_ref[...], both[...])
    out_ref[...] = refs[0][...] + total if count else total


def product(matrix, panel, index, before=(), waits=()):
    rows = matrix.shape[0]
    cols = panel.shape[0]
    tile = tile_rows(rows, 512)
    piece = pl.BlockSpec((tile, NB), lambda i: (i, 0))
    return pl.pallas_call(
        functools.partial(product_kernel, len(before)),
        grid=(rows // tile,),
        in_specs=[
            pl.BlockSpec((tile, cols), lambda i: (i, index)),
            pl.BlockSpec((cols, NB), lambda i: (0, 0)),
            *[piece for _ in before],
            *[pl.BlockSpec(memory_space=pl.ANY) for _ in waits],
        ],
        out_specs=piece,
        out_shape=jax.ShapeDtypeStruct((rows, NB), F32),
        scratch_shapes=[pltpu.VMEM((cols, 2 * NB), BF16)],
        compiler_params=pltpu.CompilerParams(vmem_limit_bytes=24 * 1024 * 1024),
        cost_estimate=pl.CostEstimate(
            flops=8 * rows * cols * NB, bytes_accessed=4 * rows * cols, transcendentals=0
        ),
        name="product",
    )(matrix, panel, *before, *waits)


def subtract_kernel(count, a_ref, *refs):
    lefts, rights = refs[:count], refs[count : 2 * count]
    out_ref, right = refs[-2:]

    @pl.when(pl.program_id(0) == 0)
    def _():
        set_right(rights, right)

    left = left_parts(lefts)
    cols = a_ref.shape[1]
    step = column_step(cols)
    for first in range(0, cols, step):
        out_ref[:, first : first + step] = less(a_ref, left, right, first, step)


def subtract(matrix, index, left, right, into=()):
    rows = matrix.shape[0]
    cols = right[0].shape[0]
    count = len(left)
    tile = tile_rows(rows, 256)
    block = pl.BlockSpec((tile, cols), lambda i: (i, index))
    return pl.pallas_call(
        functools.partial(subtract_kernel, count),
        grid=(rows // tile,),
        in_specs=[
            block,
            *[pl.BlockSpec((tile, NB), lambda i: (i, 0))] * count,
            *[pl.BlockSpec((cols, NB), lambda i: (0, 0))] * count,
            *[pl.BlockSpec(memory_space=pl.ANY) for _ in into],
        ],
        out_specs=block,
        out_shape=jax.ShapeDtypeStruct(matrix.shape, F32),
        scratch_shapes=[pltpu.VMEM((cols, 3 * count * NB), BF16)],
        input_output_aliases={2 * count + 1: 0} if into else {},
        compiler_params=pltpu.CompilerParams(vmem_limit_bytes=36 * 1024 * 1024),
        cost_estimate=pl.CostEstimate(
            flops=6 * count * rows * cols * NB, bytes_accessed=8 * rows * cols, transcendentals=0
        ),
        name="subtract",
    )(matrix, *left, *right, *into)


def factor_kernel(gram_ref, *refs):
    out_ref, rest, side = refs[-3:]
    rest[...] = gram_ref[...]
    down = lax.broadcasted_iota(jnp.int32, (NB, NB), 0)
    side[...] = jnp.where(down == lax.broadcasted_iota(jnp.int32, (NB, NB), 1), 1.0, 0.0)
    for first in range(0, NB, GROUP):
        end = first + GROUP
        rows = [rest[i : i + 1, :] for i in range(first, end)]
        sides = [side[i : i + 1, :] for i in range(first, end)]
        corner = {
            (i, j): jnp.broadcast_to(rows[i][:, first + j : first + j + 1], (1, NB))
            for i in range(GROUP)
            for j in range(i + 1)
        }
        for j in range(GROUP):
            pivot = corner[j, j]
            scale = lax.rsqrt(pivot)
            scale = scale * (1.5 - 0.5 * pivot * scale * scale)
            rows[j] = rows[j] * scale
            sides[j] = sides[j] * scale
            low = {i: corner[i, j] * scale for i in range(j + 1, GROUP)}
            for i in range(j + 1, GROUP):
                rows[i] = rows[i] - low[i] * rows[j]
                sides[i] = sides[i] - low[i] * sides[j]
                for k in range(j + 1, i + 1):
                    corner[i, k] = corner[i, k] - low[i] * low[k]
        upper = jnp.concatenate(rows, axis=0)
        inverse = jnp.concatenate(sides, axis=0)
        side[first:end, :] = inverse
        if end < NB:
            taken = contract(upper, jnp.concatenate([upper, inverse], axis=1), 0, 0)
            rest[end:, :] = rest[end:, :] - taken[end:, :NB]
            side[end:, :] = side[end:, :] - taken[end:, NB:]
    out_ref[...] = side[...].T


def inverse_factor(gram, waits=()):
    return pl.pallas_call(
        factor_kernel,
        in_specs=[pl.BlockSpec((NB, NB), lambda: (0, 0)), *[pl.BlockSpec(memory_space=pl.ANY) for _ in waits]],
        out_shape=jax.ShapeDtypeStruct((NB, NB), F32),
        scratch_shapes=[pltpu.VMEM((NB, NB), F32)] * 2,
        compiler_params=pltpu.CompilerParams(vmem_limit_bytes=16 * 1024 * 1024),
        cost_estimate=pl.CostEstimate(flops=4 * NB**3, bytes_accessed=8 * NB * NB, transcendentals=NB),
        name="factor",
    )(gram, *waits)


def after(value, *others):
    return value + jnp.float32(0.0) * sum(other[0, 0] for other in others)


class Grid:
    def __init__(self):
        self.rows = lax.axis_size("row")
        self.cols = lax.axis_size("col")
        self.row = lax.axis_index("row")
        self.col = lax.axis_index("col")
        self.width = self.cols // CORES
        self.depth = self.rows // self.width
        self.sources = self.rows // self.cols
        self.z = self.row // self.width
        self.x = self.row % self.width

    def device(self, z, x, col):
        return (z * self.width + x) * self.cols + col

    def send(self, value, pairs):
        return lax.ppermute(value, AXES, pairs)

    def swap(self, value, axis, bit):
        size = lax.axis_size(axis)
        return lax.ppermute(value, axis, [(i, i ^ bit) for i in range(size)])

    def add_over(self, value, axis, bit):
        while bit < lax.axis_size(axis):
            value = value + self.swap(value, axis, bit)
            bit *= 2
        return value

    def add_all(self, value):
        value = self.add_over(self.add_over(value, "row", 1), "col", CORES)
        return value + self.swap(value, "col", 1)

    def join_cores(self, half):
        other = self.swap(half, "col", 1)
        first = self.col % CORES == 0
        return jnp.concatenate([jnp.where(first, half, other), jnp.where(first, other, half)], axis=0)

    def own_half(self, value):
        half = value.shape[0] // CORES
        return lax.dynamic_slice_in_dim(value, self.col % CORES * half, half, axis=0)

    def other_half(self, value):
        half = value.shape[0] // CORES
        return lax.dynamic_slice_in_dim(value, (1 - self.col % CORES) * half, half, axis=0)

    def sum_half(self, value, *others):
        mine = after(self.own_half(value) + self.swap(self.other_half(value), "col", 1), *others)
        return self.add_over(mine, "col", CORES), mine

    def to_all_chips(self, value):
        total = jnp.where(self.col < CORES, value, jnp.zeros_like(value))
        for pairs in self.from_zero():
            total = total + self.send(value, pairs)
        return total

    def from_zero(self):
        return [
            [
                (r * self.cols + core, r * self.cols + y * CORES + core)
                for r in range(self.rows)
                for core in range(CORES)
            ]
            for y in range(1, self.cols // CORES)
        ]

    def from_chip_zero(self, value, start=(), end=()):
        came = self.to_all_chips(after(self.own_half(value), *start))
        return self.join_cores(after(came, *end)), came

    def to_columns(self, item, chunks):
        size = item.shape[0] // chunks
        found = []
        for i in range(chunks):
            part = item[i * size : (i + 1) * size]
            if found:
                part = after(part, found[-1].first)
            found.append(Gather(self, part, found[-1].crossed if found else ()))
        return found


class Gather:
    def __init__(self, grid, item, before):
        wide, deep, cols, count = grid.width, grid.depth, grid.cols, grid.sources
        self.grid = grid

        def pairs(moves):
            found = []
            for col in range(cols):
                mirror = col // wide == 1
                for m, n in moves:
                    z, to = (deep - 1 - m, deep - 1 - n) if mirror else (m, n)
                    found.append((grid.device(z, col % wide, col), grid.device(to, col % wide, col)))
            return found

        mirror = grid.col // wide == 1
        place = jnp.where(mirror, deep - 1 - grid.z, grid.z)
        even = range(0, deep, 2)
        self.first = grid.send(item, pairs([(e, e + 1) for e in even]))
        far = {t: grid.send(item, pairs([(e, (e + 2 * t) % deep) for e in even])) for t in range(1, count)}
        self.direct = far[1]
        down = {}
        for d in range(count - 1):
            value = item if d == 0 else far[count - d]
            down[d] = grid.send(value, pairs([(e, e - 1) for e in even if e >= 2 and e + 2 * d < deep]))
        up = {t: grid.send(far[t], pairs([(e, e + 1) for e in even if e >= 2 * t])) for t in far}
        self.relative = [jnp.where(place % 2 == 0, item, after(self.first, *before[:1]))]
        self.relative += [far[t] + up[t] + after(down[count - 1 - t], *before[1:]) for t in far]
        self.distant = self.relative[1]
        self.crossed = []
        for value in self.relative:
            crossed = jnp.zeros_like(value)
            for d in range(1, wide):
                moves = [
                    (grid.device(z, col % wide, col), grid.device(z, (col + d) % wide, col))
                    for z in range(deep)
                    for col in range(cols)
                ]
                crossed = crossed + grid.send(value, moves)
            self.crossed.append(crossed)

    def columns(self, *others):
        grid, count = self.grid, self.grid.sources
        home = grid.x == grid.col % grid.width
        whole = [
            jnp.where(home, value, after(crossed, *others))
            for value, crossed in zip(self.relative, self.crossed, strict=True)
        ]
        own = grid.z // 2
        slots = []
        for j in range(count):
            t = jnp.where(grid.col // grid.width == 1, j - own, own - j) % count
            slots.append(lax.select_n(t, *whole) if count > 2 else jnp.where(t == 0, whole[0], whole[1]))
        wide = slots[0].shape[1]
        return jnp.concatenate([s.reshape(-1, 1, NB, wide) for s in slots], axis=1).reshape(-1, wide)


def body(matrix):
    grid = Grid()
    local_rows, local_cols = matrix.shape
    chunks = 2
    width = local_cols // chunks
    row_slot = jnp.arange(local_rows, dtype=jnp.int32)
    natural_rows = ((row_slot // NB * grid.rows + grid.row) * NB + row_slot % NB)[:, None]
    zero = jnp.float32(0.0)

    def below(value, panel):
        return jnp.where(natural_rows >= (panel + 1) * NB, value, zero)

    def both(a, b):
        return jnp.concatenate([a, b], axis=0)

    mine = matrix[:, :NB]
    other = grid.swap(mine, "col", 1)
    first = grid.col % CORES == 0
    p0, came = grid.from_chip_zero(below(jnp.where(first, mine, other), 0))
    gather = grid.to_columns(p0, chunks)
    b1, _ = grid.from_chip_zero(jnp.where(first, other, mine), (came,))

    p0c = []
    y0 = ()
    for i in range(chunks):
        p0c.append(gather[i].columns(*y0))
        y0 = (product(matrix, p0c[i], i, y0),)
    gram = contract(p0c[0], p0c[0], 0, 0) + contract(p0c[1], p0c[1], 0, 0)
    small = both(gram, jnp.where(grid.col == 1, p0c[0][:NB], zero))
    small = small + grid.swap(small, "col", 1)
    small = grid.add_over(after(small, y0[0]), "col", CORES)
    gram0, p0_one = small[:NB], small[NB:]
    half, part = grid.sum_half(y0[0])
    corner = jnp.where((grid.row == 1) & first, part[:NB], zero)
    small = grid.add_all(both(contract(grid.own_half(p0) * SCALE, part, 0, 0), corner))
    t0 = inverse_factor(gram0, (part,))
    y0 = grid.join_cores(half)
    w0 = contract(p0, t0, 1, 0)
    w0_one = contract(p0_one, t0, 1, 0)
    m0, y0_one = contract(contract(t0 / SCALE, small[:NB], 0, 0), t0, 1, 0), small[NB:]

    def coupled(w, y):
        return 2.0 * contract(t0, y, 0, 0) - 4.0 * contract(m0, w, 1, 0), 2.0 * contract(t0, w, 1, 0)

    for_w, for_y = coupled(w0_one.T, y0_one.T)
    p1 = below(b1 - contract(w0, for_w, 1, 0) - contract(y0, for_y, 1, 0), 1)
    gather = grid.to_columns(p1, chunks)
    (gather_y,) = grid.to_columns(after(y0, gather[-1].distant), 1)
    w0c = [contract(part, t0, 1, 0) for part in p0c]
    p1c = []
    r1 = ()
    waits = ((), (gather_y.first,))
    for i in range(chunks):
        p1c.append(gather[i].columns(*r1))
        r1 = (product(matrix, p1c[i], i, r1, waits[i]),)
    small = sum(both(contract(p1c[i], p1c[i], 0, 0), contract(w0c[i], p1c[i], 0, 0)) for i in range(chunks))
    small = small + grid.swap(small, "col", 1)
    small = grid.add_over(after(small, r1[0]), "col", CORES)
    gram1, w_p = small[:NB], small[NB:]
    half, part = grid.sum_half(r1[0], gather_y.direct)
    sides = jnp.concatenate([grid.own_half(p1), grid.own_half(p0)], axis=1) * SCALE
    small = grid.add_all(contract(sides, part, 0, 0))
    t1 = inverse_factor(gram1, (part,))
    r1 = grid.join_cores(after(half, gather_y.distant, gather_y.crossed[0]))
    gather = grid.to_columns(r1, chunks)

    y_p = small[NB:] / SCALE
    back_w, back_y = coupled(w_p, y_p)
    taken = contract(w_p, back_w, 0, 0) + contract(y_p, back_y, 0, 0)
    m1 = contract(contract(t1 / SCALE, small[:NB] - SCALE * taken, 0, 0), t1, 1, 0)
    y1 = r1 - contract(w0, back_w, 1, 0) - contract(y0, back_y, 1, 0)
    w1 = contract(p1, t1, 1, 0)
    x1 = contract(y1, t1, 1, 0)
    for_r = 2.0 * contract(w1, t1, 1, 1)
    for_p = contract(2.0 * x1 - 4.0 * contract(w1, m1, 1, 0), t1, 1, 1)
    to_w = 2.0 * contract(y0, t0, 1, 0) - 4.0 * contract(w0, m0, 1, 0) - contract(for_r, back_w, 1, 1)
    to_y = 2.0 * contract(w0, t0, 1, 1) - contract(for_r, back_y, 1, 1)
    y0c = gather_y.columns()
    updated = ()
    for i in range(chunks):
        rights = (w0c[i], y0c[i * width : (i + 1) * width], p1c[i], gather[i].columns(*updated))
        updated = (subtract(matrix, i, (to_w, to_y, for_p, for_r), rights, updated),)
    return updated[0]


def solution(mesh):
    placed = (P("row", "col"),)
    return jax.shard_map(
        body, mesh=mesh, in_specs=placed, out_specs=P("row", "col"), check_vma=False
    )
```

```python
import functools

import jax
import jax.numpy as jnp
from jax import lax
from jax.experimental import pallas as pl
from jax.experimental.pallas import tpu as pltpu
from jax.sharding import PartitionSpec as P

NB = 128
PANELS = 2
CORES = 2
GROUP = 8
SCALE = 2.0**60
HIGH = lax.Precision.HIGHEST
BF16 = jnp.bfloat16
F32 = jnp.float32
AXES = ("row", "col")


def contract(left, right, left_dim, right_dim):
    return lax.dot_general(left, right, (((left_dim,), (right_dim,)), ((), ())), precision=HIGH)


def tile_rows(rows, most):
    return most if rows % most == 0 else rows


def halves(value):
    high = value.astype(BF16)
    return high, (value - high.astype(F32)).astype(BF16)


def set_panel(ref, both):
    high, low = halves(ref[...])
    both[:, :NB] = high
    both[:, NB:] = low


def set_right(refs, right):
    for place, ref in enumerate(refs):
        high, low = halves(ref[...])
        first = 3 * place * NB
        right[:, first : first + NB] = high
        right[:, first + NB : first + 2 * NB] = low
        right[:, first + 2 * NB : first + 3 * NB] = high


def left_parts(refs):
    parts = []
    for ref in refs:
        high, low = halves(ref[...])
        parts += [high, high, low]
    return jnp.concatenate(parts, axis=1)


def less(a_ref, left, right, first, step):
    part = lax.dot_general(
        left, right[first : first + step, :], (((1,), (1,)), ((), ())), preferred_element_type=F32
    )
    return a_ref[:, first : first + step] - part


def times(a, p):
    high, low = halves(a)
    total = jnp.dot(high, p, preferred_element_type=F32) + jnp.dot(low, p, preferred_element_type=F32)
    return total[:, :NB] + total[:, NB:]


def column_step(cols):
    return 512 if cols % 512 == 0 else cols


def crossed_gram(left, right):
    parts = lax.dot_general(left, right, (((0,), (0,)), ((), ())), preferred_element_type=F32)
    return parts[:NB, :NB] + parts[:NB, NB:] + parts[NB:, :NB] + parts[NB:, NB:]


def product_kernel(count, sides, a_ref, p_ref, *refs):
    out_ref, gram_ref, both, other = refs[-4:]

    @pl.when(pl.program_id(0) == 0)
    def _():
        set_panel(p_ref, both)
        gram_ref[:NB, :] = crossed_gram(both[...], both[...])
        for i, side in enumerate(refs[count : count + sides]):
            set_panel(side, other)
            gram_ref[(i + 1) * NB : (i + 2) * NB, :] = crossed_gram(other[...], both[...])

    total = times(a_ref[...], both[...])
    out_ref[...] = refs[0][...] + total if count else total


def product(matrix, panel, index, before=(), sides=(), waits=()):
    rows = matrix.shape[0]
    cols = panel.shape[0]
    tile = tile_rows(rows, 512)
    piece = pl.BlockSpec((tile, NB), lambda i: (i, 0))
    whole = pl.BlockSpec((cols, NB), lambda i: (0, 0))
    count = 1 + len(sides)
    return pl.pallas_call(
        functools.partial(product_kernel, len(before), len(sides)),
        grid=(rows // tile,),
        in_specs=[
            pl.BlockSpec((tile, cols), lambda i: (i, index)),
            whole,
            *[piece for _ in before],
            *[whole for _ in sides],
            *[pl.BlockSpec(memory_space=pl.ANY) for _ in waits],
        ],
        out_specs=[piece, pl.BlockSpec((count * NB, NB), lambda i: (0, 0))],
        out_shape=[jax.ShapeDtypeStruct((rows, NB), F32), jax.ShapeDtypeStruct((count * NB, NB), F32)],
        scratch_shapes=[pltpu.VMEM((cols, 2 * NB), BF16)] * 2,
        compiler_params=pltpu.CompilerParams(vmem_limit_bytes=28 * 1024 * 1024),
        cost_estimate=pl.CostEstimate(
            flops=8 * rows * cols * NB, bytes_accessed=4 * rows * cols, transcendentals=0
        ),
        name="product",
    )(matrix, panel, *before, *sides, *waits)


def subtract_kernel(count, a_ref, *refs):
    lefts, rights = refs[:count], refs[count : 2 * count]
    out_ref, right = refs[-2:]

    @pl.when(pl.program_id(0) == 0)
    def _():
        set_right(rights, right)

    left = left_parts(lefts)
    cols = a_ref.shape[1]
    step = column_step(cols)
    for first in range(0, cols, step):
        out_ref[:, first : first + step] = less(a_ref, left, right, first, step)


def subtract(matrix, index, left, right, into=()):
    rows = matrix.shape[0]
    cols = right[0].shape[0]
    count = len(left)
    tile = tile_rows(rows, 256)
    block = pl.BlockSpec((tile, cols), lambda i: (i, index))
    return pl.pallas_call(
        functools.partial(subtract_kernel, count),
        grid=(rows // tile,),
        in_specs=[
            block,
            *[pl.BlockSpec((tile, NB), lambda i: (i, 0))] * count,
            *[pl.BlockSpec((cols, NB), lambda i: (0, 0))] * count,
            *[pl.BlockSpec(memory_space=pl.ANY) for _ in into],
        ],
        out_specs=block,
        out_shape=jax.ShapeDtypeStruct(matrix.shape, F32),
        scratch_shapes=[pltpu.VMEM((cols, 3 * count * NB), BF16)],
        input_output_aliases={2 * count + 1: 0} if into else {},
        compiler_params=pltpu.CompilerParams(vmem_limit_bytes=36 * 1024 * 1024),
        cost_estimate=pl.CostEstimate(
            flops=6 * count * rows * cols * NB, bytes_accessed=8 * rows * cols, transcendentals=0
        ),
        name="subtract",
    )(matrix, *left, *right, *into)


def factor_kernel(gram_ref, *refs):
    out_ref, rest, side = refs[-3:]
    rest[...] = gram_ref[...]
    down = lax.broadcasted_iota(jnp.int32, (NB, NB), 0)
    side[...] = jnp.where(down == lax.broadcasted_iota(jnp.int32, (NB, NB), 1), 1.0, 0.0)
    for first in range(0, NB, GROUP):
        end = first + GROUP
        rows = [rest[i : i + 1, :] for i in range(first, end)]
        sides = [side[i : i + 1, :] for i in range(first, end)]
        corner = {
            (i, j): jnp.broadcast_to(rows[i][:, first + j : first + j + 1], (1, NB))
            for i in range(GROUP)
            for j in range(i + 1)
        }
        for j in range(GROUP):
            pivot = corner[j, j]
            scale = lax.rsqrt(pivot)
            scale = scale * (1.5 - 0.5 * pivot * scale * scale)
            rows[j] = rows[j] * scale
            sides[j] = sides[j] * scale
            low = {i: corner[i, j] * scale for i in range(j + 1, GROUP)}
            for i in range(j + 1, GROUP):
                rows[i] = rows[i] - low[i] * rows[j]
                sides[i] = sides[i] - low[i] * sides[j]
                for k in range(j + 1, i + 1):
                    corner[i, k] = corner[i, k] - low[i] * low[k]
        upper = jnp.concatenate(rows, axis=0)
        inverse = jnp.concatenate(sides, axis=0)
        side[first:end, :] = inverse
        if end < NB:
            taken = contract(upper, jnp.concatenate([upper, inverse], axis=1), 0, 0)
            rest[end:, :] = rest[end:, :] - taken[end:, :NB]
            side[end:, :] = side[end:, :] - taken[end:, NB:]
    out_ref[...] = side[...].T


def inverse_factor(gram, waits=()):
    return pl.pallas_call(
        factor_kernel,
        in_specs=[pl.BlockSpec((NB, NB), lambda: (0, 0)), *[pl.BlockSpec(memory_space=pl.ANY) for _ in waits]],
        out_shape=jax.ShapeDtypeStruct((NB, NB), F32),
        scratch_shapes=[pltpu.VMEM((NB, NB), F32)] * 2,
        compiler_params=pltpu.CompilerParams(vmem_limit_bytes=16 * 1024 * 1024),
        cost_estimate=pl.CostEstimate(flops=4 * NB**3, bytes_accessed=8 * NB * NB, transcendentals=NB),
        name="factor",
    )(gram, *waits)


def after(value, *others):
    return value + jnp.float32(0.0) * sum(other[0, 0] for other in others)


class Grid:
    def __init__(self):
        self.rows = lax.axis_size("row")
        self.cols = lax.axis_size("col")
        self.row = lax.axis_index("row")
        self.col = lax.axis_index("col")
        self.width = self.cols // CORES
        self.depth = self.rows // self.width
        self.sources = self.rows // self.cols
        self.z = self.row // self.width
        self.x = self.row % self.width

    def device(self, z, x, col):
        return (z * self.width + x) * self.cols + col

    def send(self, value, pairs):
        return lax.ppermute(value, AXES, pairs)

    def swap(self, value, axis, bit):
        size = lax.axis_size(axis)
        return lax.ppermute(value, axis, [(i, i ^ bit) for i in range(size)])

    def add_over(self, value, axis, bit):
        while bit < lax.axis_size(axis):
            value = value + self.swap(value, axis, bit)
            bit *= 2
        return value

    def add_chips(self, value):
        return self.add_over(value + self.swap(value, "col", 1), "col", CORES)

    def join_cores(self, half):
        other = self.swap(half, "col", 1)
        first = self.col % CORES == 0
        return jnp.concatenate([jnp.where(first, half, other), jnp.where(first, other, half)], axis=0)

    def own_half(self, value):
        half = value.shape[0] // CORES
        return lax.dynamic_slice_in_dim(value, self.col % CORES * half, half, axis=0)

    def other_half(self, value):
        half = value.shape[0] // CORES
        return lax.dynamic_slice_in_dim(value, (1 - self.col % CORES) * half, half, axis=0)

    def sum_half(self, value, *others):
        mine = after(self.own_half(value) + self.swap(self.other_half(value), "col", 1), *others)
        return self.add_over(mine, "col", CORES), mine

    def to_all_chips(self, value):
        total = jnp.where(self.col < CORES, value, jnp.zeros_like(value))
        for pairs in self.from_zero():
            total = total + self.send(value, pairs)
        return total

    def from_zero(self):
        return [
            [
                (r * self.cols + core, r * self.cols + y * CORES + core)
                for r in range(self.rows)
                for core in range(CORES)
            ]
            for y in range(1, self.cols // CORES)
        ]

    def from_chip_zero(self, value, start=(), end=()):
        came = self.to_all_chips(after(self.own_half(value), *start))
        return self.join_cores(after(came, *end)), came

    def to_columns(self, item, chunks):
        size = item.shape[0] // chunks
        return [Gather(self, item[i * size : (i + 1) * size]) for i in range(chunks)]


class Gather:
    def __init__(self, grid, item):
        wide, deep, cols, count = grid.width, grid.depth, grid.cols, grid.sources
        self.grid = grid

        def pairs(moves):
            found = []
            for col in range(cols):
                mirror = col // wide == 1
                for m, n in moves:
                    z, to = (deep - 1 - m, deep - 1 - n) if mirror else (m, n)
                    found.append((grid.device(z, col % wide, col), grid.device(to, col % wide, col)))
            return found

        mirror = grid.col // wide == 1
        place = jnp.where(mirror, deep - 1 - grid.z, grid.z)
        even = range(0, deep, 2)
        self.first = grid.send(item, pairs([(e, e + 1) for e in even]))
        far = {t: grid.send(item, pairs([(e, (e + 2 * t) % deep) for e in even])) for t in range(1, count)}
        self.direct = far[1]
        down = {}
        for d in range(count - 1):
            value = item if d == 0 else far[count - d]
            down[d] = grid.send(value, pairs([(e, e - 1) for e in even if e >= 2 and e + 2 * d < deep]))
        up = {t: grid.send(far[t], pairs([(e, e + 1) for e in even if e >= 2 * t])) for t in far}
        self.relative = [jnp.where(place % 2 == 0, item, self.first)]
        self.relative += [far[t] + up[t] + down[count - 1 - t] for t in far]
        self.distant = self.relative[1]
        self.crossed = []
        for value in self.relative:
            crossed = jnp.zeros_like(value)
            for d in range(1, wide):
                moves = [
                    (grid.device(z, col % wide, col), grid.device(z, (col + d) % wide, col))
                    for z in range(deep)
                    for col in range(cols)
                ]
                crossed = crossed + grid.send(value, moves)
            self.crossed.append(crossed)

    def columns(self, *others):
        grid, count = self.grid, self.grid.sources
        home = grid.x == grid.col % grid.width
        whole = [
            jnp.where(home, value, after(crossed, *others))
            for value, crossed in zip(self.relative, self.crossed, strict=True)
        ]
        own = grid.z // 2
        slots = []
        for j in range(count):
            t = jnp.where(grid.col // grid.width == 1, j - own, own - j) % count
            slots.append(lax.select_n(t, *whole) if count > 2 else jnp.where(t == 0, whole[0], whole[1]))
        wide = slots[0].shape[1]
        return jnp.concatenate([s.reshape(-1, 1, NB, wide) for s in slots], axis=1).reshape(-1, wide)


def body(matrix):
    grid = Grid()
    local_rows, local_cols = matrix.shape
    chunks = 2
    width = local_cols // chunks
    row_slot = jnp.arange(local_rows, dtype=jnp.int32)
    natural_rows = ((row_slot // NB * grid.rows + grid.row) * NB + row_slot % NB)[:, None]
    zero = jnp.float32(0.0)

    def below(value, panel):
        return jnp.where(natural_rows >= (panel + 1) * NB, value, zero)

    def both(a, b):
        return jnp.concatenate([a, b], axis=0)

    mine = matrix[:, :NB]
    other = grid.swap(mine, "col", 1)
    first = grid.col % CORES == 0
    p0, came = grid.from_chip_zero(below(jnp.where(first, mine, other), 0))
    gather = grid.to_columns(p0, chunks)
    b1, _ = grid.from_chip_zero(jnp.where(first, other, mine), (came,))

    p0c, grams = [], []
    y0 = ()
    for i in range(chunks):
        p0c.append(gather[i].columns(*y0))
        part, gram = product(matrix, p0c[i], i, y0)
        grams.append(gram)
        y0 = (part,)
    small = both(sum(grams), jnp.where(grid.col == 1, p0c[0][:NB], zero))
    small = grid.add_chips(small)
    gram0, p0_one = small[:NB], small[NB:]
    half, part = grid.sum_half(y0[0])
    corner = jnp.where((grid.row == 1) & first, part[:NB], zero)
    small = both(contract(grid.own_half(p0) * SCALE, part, 0, 0), corner)
    small = grid.add_chips(grid.add_over(small, "row", 1))
    t0 = inverse_factor(gram0, (part,))
    y0 = grid.join_cores(half)

    w0_one = contract(p0_one, t0, 1, 0)
    for_y = 2.0 * contract(t0, w0_one, 1, 1)
    rest = below(b1 - contract(y0, for_y, 1, 0), 1)
    m0, y0_one = contract(contract(t0 / SCALE, small[:NB], 0, 0), t0, 1, 0), small[NB:]
    w0 = contract(p0, t0, 1, 0)
    w0c = [contract(part, t0, 1, 0) for part in p0c]

    def coupled(w, y):
        return 2.0 * contract(t0, y, 0, 0) - 4.0 * contract(m0, w, 1, 0), 2.0 * contract(t0, w, 1, 0)

    for_w, _ = coupled(w0_one.T, y0_one.T)
    p1 = rest - below(contract(w0, for_w, 1, 0), 1)
    gather = grid.to_columns(p1, chunks)
    (gather_y,) = grid.to_columns(after(y0, gather[-1].distant), 1)
    waits = ((), (gather_y.first,))
    p1c, grams = [], []
    r1 = ()
    for i in range(chunks):
        p1c.append(gather[i].columns(*r1))
        part, gram = product(matrix, p1c[i], i, r1, (p0c[i],), waits[i])
        grams.append(gram)
        r1 = (part,)
    half, part = grid.sum_half(r1[0], gather_y.direct)
    sides = jnp.concatenate([grid.own_half(p1), grid.own_half(p0)], axis=1) * SCALE
    small = grid.add_chips(grid.add_over(contract(sides, part, 0, 0), "row", 1))
    grams = grid.add_chips(sum(grams))
    gram1, w_p = grams[:NB], contract(t0, grams[NB:], 0, 0)
    t1 = inverse_factor(gram1, (part,))
    r1 = grid.join_cores(after(half, gather_y.distant, gather_y.crossed[0]))
    gather = grid.to_columns(r1, chunks)

    y_p = small[NB:] / SCALE
    back_w, back_y = coupled(w_p, y_p)
    taken = contract(w_p, back_w, 0, 0) + contract(y_p, back_y, 0, 0)
    m1 = contract(contract(t1 / SCALE, small[:NB] - SCALE * taken, 0, 0), t1, 1, 0)
    y1 = r1 - contract(w0, back_w, 1, 0) - contract(y0, back_y, 1, 0)
    w1 = contract(p1, t1, 1, 0)
    x1 = contract(y1, t1, 1, 0)
    for_r = 2.0 * contract(w1, t1, 1, 1)
    for_p = contract(2.0 * x1 - 4.0 * contract(w1, m1, 1, 0), t1, 1, 1)
    to_w = 2.0 * contract(y0, t0, 1, 0) - 4.0 * contract(w0, m0, 1, 0) - contract(for_r, back_w, 1, 1)
    to_y = 2.0 * contract(w0, t0, 1, 1) - contract(for_r, back_y, 1, 1)
    y0c = gather_y.columns()
    updated = ()
    for i in range(chunks):
        rights = (w0c[i], y0c[i * width : (i + 1) * width], p1c[i], gather[i].columns(*updated))
        updated = (subtract(matrix, i, (to_w, to_y, for_p, for_r), rights, updated),)
    return updated[0]


def solution(mesh):
    placed = (P("row", "col"),)
    return jax.shard_map(
        body, mesh=mesh, in_specs=placed, out_specs=P("row", "col"), check_vma=False
    )
```

```python
import functools

import jax
import jax.numpy as jnp
from jax import lax
from jax.experimental import pallas as pl
from jax.experimental.pallas import tpu as pltpu
from jax.sharding import PartitionSpec as P

NB = 128
PANELS = 2
CORES = 2
GROUP = 8
SCALE = 2.0**60
HIGH = lax.Precision.HIGHEST
BF16 = jnp.bfloat16
F32 = jnp.float32
AXES = ("row", "col")


def contract(left, right, left_dim, right_dim):
    return lax.dot_general(left, right, (((left_dim,), (right_dim,)), ((), ())), precision=HIGH)


def tile_rows(rows, most):
    return most if rows % most == 0 else rows


def halves(value):
    high = value.astype(BF16)
    return high, (value - high.astype(F32)).astype(BF16)


def set_panel(ref, both):
    high, low = halves(ref[...])
    both[:, :NB] = high
    both[:, NB:] = low


def set_right(refs, right):
    for place, ref in enumerate(refs):
        high, low = halves(ref[...])
        first = 3 * place * NB
        right[:, first : first + NB] = high
        right[:, first + NB : first + 2 * NB] = low
        right[:, first + 2 * NB : first + 3 * NB] = high


def left_parts(refs):
    parts = []
    for ref in refs:
        high, low = halves(ref[...])
        parts += [high, high, low]
    return jnp.concatenate(parts, axis=1)


def less(a_ref, left, right, first, step):
    part = lax.dot_general(
        left, right[first : first + step, :], (((1,), (1,)), ((), ())), preferred_element_type=F32
    )
    return a_ref[:, first : first + step] - part


def times(a, p):
    high, low = halves(a)
    total = jnp.dot(high, p, preferred_element_type=F32) + jnp.dot(low, p, preferred_element_type=F32)
    return total[:, :NB] + total[:, NB:]


def column_step(cols):
    return 512 if cols % 512 == 0 else cols


def crossed_gram(left, right):
    parts = lax.dot_general(left, right, (((0,), (0,)), ((), ())), preferred_element_type=F32)
    return parts[:NB, :NB] + parts[:NB, NB:] + parts[NB:, :NB] + parts[NB:, NB:]


def product_kernel(count, sides, a_ref, p_ref, *refs):
    out_ref, gram_ref, both, other = refs[-4:]

    @pl.when(pl.program_id(0) == 0)
    def _():
        set_panel(p_ref, both)
        gram_ref[:NB, :] = crossed_gram(both[...], both[...])
        for i, side in enumerate(refs[count : count + sides]):
            set_panel(side, other)
            gram_ref[(i + 1) * NB : (i + 2) * NB, :] = crossed_gram(other[...], both[...])

    total = times(a_ref[...], both[...])
    out_ref[...] = refs[0][...] + total if count else total


def product(matrix, panel, index, before=(), sides=(), waits=()):
    rows = matrix.shape[0]
    cols = panel.shape[0]
    tile = tile_rows(rows, 512)
    piece = pl.BlockSpec((tile, NB), lambda i: (i, 0))
    whole = pl.BlockSpec((cols, NB), lambda i: (0, 0))
    count = 1 + len(sides)
    return pl.pallas_call(
        functools.partial(product_kernel, len(before), len(sides)),
        grid=(rows // tile,),
        in_specs=[
            pl.BlockSpec((tile, cols), lambda i: (i, index)),
            whole,
            *[piece for _ in before],
            *[whole for _ in sides],
            *[pl.BlockSpec(memory_space=pl.ANY) for _ in waits],
        ],
        out_specs=[piece, pl.BlockSpec((count * NB, NB), lambda i: (0, 0))],
        out_shape=[jax.ShapeDtypeStruct((rows, NB), F32), jax.ShapeDtypeStruct((count * NB, NB), F32)],
        scratch_shapes=[pltpu.VMEM((cols, 2 * NB), BF16)] * 2,
        compiler_params=pltpu.CompilerParams(vmem_limit_bytes=28 * 1024 * 1024),
        cost_estimate=pl.CostEstimate(
            flops=8 * rows * cols * NB, bytes_accessed=4 * rows * cols, transcendentals=0
        ),
        name="product",
    )(matrix, panel, *before, *sides, *waits)


def subtract_kernel(count, a_ref, *refs):
    lefts, rights = refs[:count], refs[count : 2 * count]
    out_ref, right = refs[-2:]

    @pl.when(pl.program_id(0) == 0)
    def _():
        set_right(rights, right)

    left = left_parts(lefts)
    cols = a_ref.shape[1]
    step = column_step(cols)
    for first in range(0, cols, step):
        out_ref[:, first : first + step] = less(a_ref, left, right, first, step)


def subtract(matrix, index, left, right, into=()):
    rows = matrix.shape[0]
    cols = right[0].shape[0]
    count = len(left)
    tile = tile_rows(rows, 256)
    block = pl.BlockSpec((tile, cols), lambda i: (i, index))
    return pl.pallas_call(
        functools.partial(subtract_kernel, count),
        grid=(rows // tile,),
        in_specs=[
            block,
            *[pl.BlockSpec((tile, NB), lambda i: (i, 0))] * count,
            *[pl.BlockSpec((cols, NB), lambda i, at=index * (r.shape[0] > cols): (at, 0)) for r in right],
            *[pl.BlockSpec(memory_space=pl.ANY) for _ in into],
        ],
        out_specs=block,
        out_shape=jax.ShapeDtypeStruct(matrix.shape, F32),
        scratch_shapes=[pltpu.VMEM((cols, 3 * count * NB), BF16)],
        input_output_aliases={2 * count + 1: 0} if into else {},
        compiler_params=pltpu.CompilerParams(vmem_limit_bytes=36 * 1024 * 1024),
        cost_estimate=pl.CostEstimate(
            flops=6 * count * rows * cols * NB, bytes_accessed=8 * rows * cols, transcendentals=0
        ),
        name="subtract",
    )(matrix, *left, *right, *into)


def factor_kernel(gram_ref, *refs):
    out_ref, rest, side = refs[-3:]
    rest[...] = gram_ref[...]
    down = lax.broadcasted_iota(jnp.int32, (NB, NB), 0)
    side[...] = jnp.where(down == lax.broadcasted_iota(jnp.int32, (NB, NB), 1), 1.0, 0.0)
    for first in range(0, NB, GROUP):
        end = first + GROUP
        rows = [rest[i : i + 1, :] for i in range(first, end)]
        sides = [side[i : i + 1, :] for i in range(first, end)]
        corner = {
            (i, j): jnp.broadcast_to(rows[i][:, first + j : first + j + 1], (1, NB))
            for i in range(GROUP)
            for j in range(i + 1)
        }
        for j in range(GROUP):
            pivot = corner[j, j]
            scale = lax.rsqrt(pivot)
            scale = scale * (1.5 - 0.5 * pivot * scale * scale)
            rows[j] = rows[j] * scale
            sides[j] = sides[j] * scale
            low = {i: corner[i, j] * scale for i in range(j + 1, GROUP)}
            for i in range(j + 1, GROUP):
                rows[i] = rows[i] - low[i] * rows[j]
                sides[i] = sides[i] - low[i] * sides[j]
                for k in range(j + 1, i + 1):
                    corner[i, k] = corner[i, k] - low[i] * low[k]
        upper = jnp.concatenate(rows, axis=0)
        inverse = jnp.concatenate(sides, axis=0)
        side[first:end, :] = inverse
        if end < NB:
            taken = contract(upper, jnp.concatenate([upper, inverse], axis=1), 0, 0)
            rest[end:, :] = rest[end:, :] - taken[end:, :NB]
            side[end:, :] = side[end:, :] - taken[end:, NB:]
    out_ref[...] = side[...].T


def inverse_factor(gram, waits=()):
    return pl.pallas_call(
        factor_kernel,
        in_specs=[pl.BlockSpec((NB, NB), lambda: (0, 0)), *[pl.BlockSpec(memory_space=pl.ANY) for _ in waits]],
        out_shape=jax.ShapeDtypeStruct((NB, NB), F32),
        scratch_shapes=[pltpu.VMEM((NB, NB), F32)] * 2,
        compiler_params=pltpu.CompilerParams(vmem_limit_bytes=16 * 1024 * 1024),
        cost_estimate=pl.CostEstimate(flops=4 * NB**3, bytes_accessed=8 * NB * NB, transcendentals=NB),
        name="factor",
    )(gram, *waits)


def after(value, *others):
    return value + jnp.float32(0.0) * sum(other[0, 0] for other in others)


class Grid:
    def __init__(self):
        self.rows = lax.axis_size("row")
        self.cols = lax.axis_size("col")
        self.row = lax.axis_index("row")
        self.col = lax.axis_index("col")
        self.width = self.cols // CORES
        self.depth = self.rows // self.width
        self.sources = self.rows // self.cols
        self.z = self.row // self.width
        self.x = self.row % self.width

    def device(self, z, x, col):
        return (z * self.width + x) * self.cols + col

    def send(self, value, pairs):
        return lax.ppermute(value, AXES, pairs)

    def swap(self, value, axis, bit):
        size = lax.axis_size(axis)
        return lax.ppermute(value, axis, [(i, i ^ bit) for i in range(size)])

    def add_over(self, value, axis, bit):
        while bit < lax.axis_size(axis):
            value = value + self.swap(value, axis, bit)
            bit *= 2
        return value

    def add_chips(self, value):
        return self.add_over(value + self.swap(value, "col", 1), "col", CORES)

    def join_cores(self, half):
        other = self.swap(half, "col", 1)
        first = self.col % CORES == 0
        return jnp.concatenate([jnp.where(first, half, other), jnp.where(first, other, half)], axis=0)

    def own_half(self, value):
        half = value.shape[0] // CORES
        return lax.dynamic_slice_in_dim(value, self.col % CORES * half, half, axis=0)

    def other_half(self, value):
        half = value.shape[0] // CORES
        return lax.dynamic_slice_in_dim(value, (1 - self.col % CORES) * half, half, axis=0)

    def sum_half(self, value, *others):
        mine = after(self.own_half(value) + self.swap(self.other_half(value), "col", 1), *others)
        return self.add_over(mine, "col", CORES), mine

    def to_all_chips(self, value):
        total = jnp.where(self.col < CORES, value, jnp.zeros_like(value))
        for pairs in self.from_zero():
            total = total + self.send(value, pairs)
        return total

    def from_zero(self):
        return [
            [
                (r * self.cols + core, r * self.cols + y * CORES + core)
                for r in range(self.rows)
                for core in range(CORES)
            ]
            for y in range(1, self.cols // CORES)
        ]

    def from_chip_zero(self, value, start=(), end=()):
        came = self.to_all_chips(after(self.own_half(value), *start))
        return self.join_cores(after(came, *end)), came

    def to_columns(self, item, chunks):
        size = item.shape[0] // chunks
        return [Gather(self, item[i * size : (i + 1) * size]) for i in range(chunks)]


class Gather:
    def __init__(self, grid, item):
        wide, deep, cols, count = grid.width, grid.depth, grid.cols, grid.sources
        self.grid = grid

        def pairs(moves):
            found = []
            for col in range(cols):
                mirror = col // wide == 1
                for m, n in moves:
                    z, to = (deep - 1 - m, deep - 1 - n) if mirror else (m, n)
                    found.append((grid.device(z, col % wide, col), grid.device(to, col % wide, col)))
            return found

        mirror = grid.col // wide == 1
        place = jnp.where(mirror, deep - 1 - grid.z, grid.z)
        even = range(0, deep, 2)
        self.first = grid.send(item, pairs([(e, e + 1) for e in even]))
        far = {t: grid.send(item, pairs([(e, (e + 2 * t) % deep) for e in even])) for t in range(1, count)}
        self.direct = far[1]
        down = {}
        for d in range(count - 1):
            value = item if d == 0 else far[count - d]
            down[d] = grid.send(value, pairs([(e, e - 1) for e in even if e >= 2 and e + 2 * d < deep]))
        up = {t: grid.send(far[t], pairs([(e, e + 1) for e in even if e >= 2 * t])) for t in far}
        self.relative = [jnp.where(place % 2 == 0, item, self.first)]
        self.relative += [far[t] + up[t] + down[count - 1 - t] for t in far]
        self.distant = self.relative[1]
        self.crossed = []
        for value in self.relative:
            crossed = jnp.zeros_like(value)
            for d in range(1, wide):
                moves = [
                    (grid.device(z, col % wide, col), grid.device(z, (col + d) % wide, col))
                    for z in range(deep)
                    for col in range(cols)
                ]
                crossed = crossed + grid.send(value, moves)
            self.crossed.append(crossed)

    def columns(self, *others):
        grid, count = self.grid, self.grid.sources
        home = grid.x == grid.col % grid.width
        whole = [
            jnp.where(home, value, after(crossed, *others))
            for value, crossed in zip(self.relative, self.crossed, strict=True)
        ]
        own = grid.z // 2
        slots = []
        for j in range(count):
            t = jnp.where(grid.col // grid.width == 1, j - own, own - j) % count
            slots.append(lax.select_n(t, *whole) if count > 2 else jnp.where(t == 0, whole[0], whole[1]))
        wide = slots[0].shape[1]
        return jnp.concatenate([s.reshape(-1, 1, NB, wide) for s in slots], axis=1).reshape(-1, wide)


def body(matrix):
    grid = Grid()
    local_rows = matrix.shape[0]
    chunks = 2
    row_slot = jnp.arange(local_rows, dtype=jnp.int32)
    natural_rows = ((row_slot // NB * grid.rows + grid.row) * NB + row_slot % NB)[:, None]
    zero = jnp.float32(0.0)

    def below(value, panel):
        return jnp.where(natural_rows >= (panel + 1) * NB, value, zero)

    def both(a, b):
        return jnp.concatenate([a, b], axis=0)

    mine = matrix[:, :NB]
    other = grid.swap(mine, "col", 1)
    first = grid.col % CORES == 0
    p0, came = grid.from_chip_zero(below(jnp.where(first, mine, other), 0))
    gather = grid.to_columns(p0, chunks)
    b1, _ = grid.from_chip_zero(jnp.where(first, other, mine), (came,))

    p0c, grams = [], []
    y0 = ()
    for i in range(chunks):
        p0c.append(gather[i].columns(*y0))
        part, gram = product(matrix, p0c[i], i, y0)
        grams.append(gram)
        y0 = (part,)
    small = both(sum(grams), jnp.where(grid.col == 1, p0c[0][:NB], zero))
    small = grid.add_chips(small)
    gram0, p0_one = small[:NB], small[NB:]
    half, part = grid.sum_half(y0[0])
    corner = jnp.where((grid.row == 1) & first, part[:NB], zero)
    small = both(contract(grid.own_half(p0) * SCALE, part, 0, 0), corner)
    small = grid.add_chips(grid.add_over(small, "row", 1))
    t0 = inverse_factor(gram0, (part,))
    y0 = grid.join_cores(half)

    w0_one = contract(p0_one, t0, 1, 0)
    for_y = 2.0 * contract(t0, w0_one, 1, 1)
    rest = below(b1 - contract(y0, for_y, 1, 0), 1)
    m0, y0_one = contract(contract(t0 / SCALE, small[:NB], 0, 0), t0, 1, 0), small[NB:]
    w0 = contract(p0, t0, 1, 0)
    w0c = [contract(part, t0, 1, 0) for part in p0c]

    def coupled(w, y):
        return 2.0 * contract(t0, y, 0, 0) - 4.0 * contract(m0, w, 1, 0), 2.0 * contract(t0, w, 1, 0)

    for_w, _ = coupled(w0_one.T, y0_one.T)
    p1 = rest - below(contract(w0, for_w, 1, 0), 1)
    gather = grid.to_columns(p1, chunks)
    (gather_y,) = grid.to_columns(after(y0, gather[-1].distant), 1)
    waits = ((), (gather_y.first,))
    p1c, grams = [], []
    r1 = ()
    for i in range(chunks):
        p1c.append(gather[i].columns(*r1))
        part, gram = product(matrix, p1c[i], i, r1, (p0c[i],), waits[i])
        grams.append(gram)
        r1 = (part,)
    half, part = grid.sum_half(r1[0])
    sides = jnp.concatenate([grid.own_half(p1), grid.own_half(p0)], axis=1) * SCALE
    small = grid.add_chips(grid.add_over(contract(sides, part, 0, 0), "row", 1))
    grams = grid.add_chips(sum(grams))
    gram1, w_p = grams[:NB], contract(t0, grams[NB:], 0, 0)
    t1 = inverse_factor(gram1, (part,))
    r1 = grid.join_cores(after(half, gather_y.distant, gather_y.crossed[0]))
    gather = grid.to_columns(r1, chunks)

    y_p = small[NB:] / SCALE
    back_w, back_y = coupled(w_p, y_p)
    taken = contract(w_p, back_w, 0, 0) + contract(y_p, back_y, 0, 0)
    m1 = contract(contract(t1 / SCALE, small[:NB] - SCALE * taken, 0, 0), t1, 1, 0)
    y1 = r1 - contract(w0, back_w, 1, 0) - contract(y0, back_y, 1, 0)
    w1 = contract(p1, t1, 1, 0)
    x1 = contract(y1, t1, 1, 0)
    for_r = 2.0 * contract(w1, t1, 1, 1)
    for_p = contract(2.0 * x1 - 4.0 * contract(w1, m1, 1, 0), t1, 1, 1)
    to_w = 2.0 * contract(y0, t0, 1, 0) - 4.0 * contract(w0, m0, 1, 0) - contract(for_r, back_w, 1, 1)
    to_y = 2.0 * contract(w0, t0, 1, 1) - contract(for_r, back_y, 1, 1)
    y0c = gather_y.columns()
    updated = ()
    for i in range(chunks):
        rights = (w0c[i], y0c, p1c[i], gather[i].columns(*updated))
        updated = (subtract(matrix, i, (to_w, to_y, for_p, for_r), rights, updated),)
    return updated[0]


def solution(mesh):
    placed = (P("row", "col"),)
    return jax.shard_map(
        body, mesh=mesh, in_specs=placed, out_specs=P("row", "col"), check_vma=False
    )
```
